768 devices in a mesh: dom: 64 (over x, y, core), grp: 12 (over z).
Axes of the slice: x: 4, y: 8, z: 12, core: 2. Of those that a mesh axis runs over, the one named last changes fastest.
Arguments:
- features: bfloat16 [1572864, 256], P(('dom', 'grp')), may hold values from -6 to 6
- weight: bfloat16 [256, 256], replicated, may hold values from -0.375 to 0.375
- cotangent: bfloat16 [1572864, 256], P(('dom', 'grp')), may hold values from -6 to 6
- edge_index: int32 [1572864, 8], P(('dom', 'grp')), may hold values from 0 to 5631
- edge_weight: float32 [1572864, 8], P(('dom', 'grp')), may hold values from 0.1 to 0.6
- send_rows: int32 [49152, 32], P(('dom', 'grp')), may hold values from 0 to 2047
- counts: int32 [49152], P(('dom', 'grp')), may hold values from 1 to 32
- boundary: int32 [98304], P(('dom', 'grp')), may hold values from 0 to 2047
- skip_flags: int32 [64, 12], P('dom'), may hold values 0 or 1
- cached_panels: bfloat16 [64, 12, 128, 256], P('dom'), may hold values from -6 to 6
Outputs:
- activated: bfloat16 [1572864, 256], P(('dom', 'grp'))
- feature_grad: bfloat16 [1572864, 256], P(('dom', 'grp'))
- weight_grad: float32 [256, 256], replicated
The draws below stay inside these ranges and needn't reach their ends.
Inputs may be any that keep to these rules, and one draw needn't show every extreme that they name: `edge_index`: rows below 2048 are the device's own nodes, the next 2048 are arrived in order of sender, the rest the panels in order of owner; slots past a block's count are zero rows. `send_rows`: indices of the sender's own rows; repeats allowed. `boundary`: indices of the owner's own rows; repeats allowed.
All inputs are finite; a program needn't handle non-finite values. No bound on the sum of `skip_flags` on one device may be relied on, other than what follows from the above.
Results may differ from the reference program's by a relative error of at most 0.014.
Values may be sent and summed in bfloat16 or wider, within the bound.
No kernel may reach another device: no remote copies, remote signals or barrier semaphores. Data moves between devices by JAX's collectives and lax.ppermute only.
A program may use at most 64 MiB of HBM per device.

```python
import math
import jax
import jax.numpy as jnp
from jax import lax

H = 256
NODE_DEV = 2048
K = 8
R = 32
B = 128
NODES = 1572864
SOURCES = 5632
N_DOM = 64
N_GRP = 12


def touch_ends(entries, own_key, smallest, high):
    longest = entries.shape.index(max(entries.shape))
    spots = []
    for shift in (0, 1):
        where = [jax.random.randint(jax.random.fold_in(own_key, axis), (), 0, length) for axis, length in enumerate(entries.shape)]
        where[longest] = (where[longest] + shift) % entries.shape[longest]
        spots.append(tuple(where))
    return entries.at[spots[0]].set(smallest).at[spots[1]].set(high)


def level_of(stream_key, shape, split, low, top_value):
    def one(dim, shards_of):
        draws = jax.random.uniform(jax.random.fold_in(jax.random.fold_in(stream_key, 6), dim), (shards_of,), jnp.float32, low / len(split), top_value / len(split))
        return jnp.repeat(jnp.exp(draws), shape[dim] // shards_of).reshape((-1,) + (1,) * (len(shape) - dim - 1))

    loudness = one(*split[0])
    for cut in split[1:]:
        loudness = loudness * one(*cut)
    return loudness


def centred(stream_key, extent, scale, bound, shards=(), kind=jnp.bfloat16):
    array = scale * jax.random.normal(stream_key, extent, jnp.float32)
    if shards:
        array = array * level_of(stream_key, extent, shards, -0.22, 0.18)
    return jnp.clip(array, -bound, bound).astype(kind)


def setup_inputs(seed: int = 0) -> dict:
    key_list = jax.random.split(jax.random.key(seed), 11)
    return {
        "features": centred(key_list[0], (NODES, H), 1.0, 6.0, ((0, 768),)),
        "weight": centred(key_list[1], (H, H), H ** -0.5, 0.375),
        "cotangent": centred(key_list[2], (NODES, H), 1.0, 6.0, ((0, 768),)),
        "edge_index": touch_ends(jax.random.randint(key_list[3], (NODES, K), 0, SOURCES), jax.random.fold_in(key_list[3], 1), 0, SOURCES - 1).astype(jnp.int32),
        "edge_weight": jnp.clip(jnp.exp(math.log(0.6) - 1.7917595 * jax.random.uniform(key_list[4], (NODES, K), jnp.float32) ** level_of(key_list[4], (NODES, K), ((0, 768),), -0.2, 0.2)), 0.1, 0.6),
        "send_rows": touch_ends(jax.random.randint(key_list[5], (NODES // NODE_DEV * N_DOM, R), 0, NODE_DEV), jax.random.fold_in(key_list[5], 1), 0, NODE_DEV - 1).astype(jnp.int32),
        "counts": touch_ends(jax.random.randint(key_list[6], (NODES // NODE_DEV * N_DOM,), 1, R + 1), jax.random.fold_in(key_list[6], 1), 1, R).astype(jnp.int32),
        "boundary": touch_ends(jax.random.randint(key_list[7], (NODES // NODE_DEV * B,), 0, NODE_DEV), jax.random.fold_in(key_list[7], 1), 0, NODE_DEV - 1).astype(jnp.int32),
        "skip_flags": touch_ends((jax.random.randint(key_list[8], (N_DOM, N_GRP), 0, 2) < 1).astype(jnp.int32), jax.random.fold_in(key_list[8], 1), 0, 1),
        "cached_panels": centred(key_list[9], (N_DOM, N_GRP, B, H), 1.0, 6.0, ((0, 64),)),
    }


def activation(values):
    return jax.nn.gelu(values, approximate=True)

def aggregate(source_table, edges_here, weights_here):
    picked = source_table[edges_here].astype(jnp.float32)
    return lax.optimization_barrier(jnp.sum(weights_here[:, :, None] * picked, axis=1))

def spread_back(grad_pre, edges_here, weights_here, table_rows):
    contrib = weights_here[:, :, None] * grad_pre[:, None, :].astype(jnp.float32)
    start_rows = jnp.zeros((table_rows, grad_pre.shape[1]), jnp.float32)
    return start_rows.at[edges_here.reshape(-1)].add(contrib.reshape(-1, grad_pre.shape[1]))

def reference(features, weight, cotangent, edge_index, edge_weight, send_rows, counts, boundary, skip_flags, cached_panels):
    devices_all = N_DOM * N_GRP
    remote_end = NODE_DEV + N_DOM * R
    table_rows = remote_end + N_GRP * B
    node_blocks = features.reshape(devices_all, NODE_DEV, H)
    projected = lax.map(lambda block_rows: jnp.dot(block_rows, weight, preferred_element_type=jnp.float32).astype(jnp.bfloat16), node_blocks)
    sends = send_rows.reshape(devices_all, N_DOM, R)
    live_slots = jnp.arange(R, dtype=jnp.int32)[None, None, :] < counts.reshape(devices_all, N_DOM)[:, :, None]
    outgoing = jax.vmap(lambda rows_here, picks: rows_here[picks])(projected, sends)
    outgoing = jnp.where(live_slots[..., None], outgoing, jnp.zeros((), jnp.bfloat16))
    arrived = outgoing.reshape(N_DOM, N_GRP, N_DOM, R, H).transpose(2, 1, 0, 3, 4).reshape(devices_all, N_DOM * R, H)
    fresh = jax.vmap(lambda rows_here, picks: rows_here[picks])(projected, boundary.reshape(devices_all, B))
    skipped = skip_flags == 1
    panels = jnp.where(skipped[:, :, None, None], cached_panels, fresh.reshape(N_DOM, N_GRP, B, H))
    edges_all = edge_index.reshape(devices_all, NODE_DEV, K)
    weights_all = edge_weight.reshape(devices_all, NODE_DEV, K)

    def first_pass(inputs):
        device, own_rows, incoming, edges_here, weights_here, cot_here = inputs
        dom_index = device // N_GRP
        source_table = jnp.concatenate([own_rows, incoming, panels[dom_index].reshape(N_GRP * B, H)], axis=0)
        preact = aggregate(source_table, edges_here, weights_here)
        activated = activation(preact).astype(jnp.bfloat16)
        _, pullback = jax.vjp(activation, preact)
        grad_pre = pullback(cot_here.astype(jnp.float32))[0].astype(jnp.bfloat16)
        table_grad = spread_back(grad_pre, edges_here, weights_here, table_rows)
        remote_grad = table_grad[NODE_DEV:remote_end].reshape(N_DOM, R, H).astype(jnp.bfloat16)
        panel_grad = jnp.where(skipped[dom_index][:, None, None], 0.0, table_grad[remote_end:].reshape(N_GRP, B, H)).astype(jnp.bfloat16)
        return (activated, grad_pre, remote_grad, panel_grad)
    device_ids = jnp.arange(devices_all, dtype=jnp.int32)
    activated, grad_pres, remote_grads, panel_grads = lax.map(first_pass, (device_ids, projected, arrived, edges_all, weights_all, cotangent.reshape(devices_all, NODE_DEV, H)))
    returned = remote_grads.reshape(N_DOM, N_GRP, N_DOM, R, H).transpose(2, 1, 0, 3, 4).reshape(devices_all, N_DOM, R, H)
    owner_grad = lax.optimization_barrier(jnp.sum(panel_grads.reshape(N_DOM, N_GRP, N_GRP, B, H).astype(jnp.float32), axis=1)).reshape(devices_all, B, H)

    def second_pass(running, inputs):
        grad_pre, edges_here, weights_here, own_features, picks, live_here, back_rows, panel_picks, panel_back = inputs
        table_grad = spread_back(grad_pre, edges_here, weights_here, table_rows)
        back_terms = jnp.where(live_here[:, :, None], back_rows.astype(jnp.float32), 0.0)
        local_grad = table_grad[:NODE_DEV].at[picks.reshape(-1)].add(back_terms.reshape(N_DOM * R, H))
        local_grad = local_grad.at[panel_picks].add(panel_back)
        grad_proj = local_grad.astype(jnp.bfloat16)
        feature_grad = jnp.dot(grad_proj, weight.T, preferred_element_type=jnp.float32).astype(jnp.bfloat16)
        weight_term = lax.dot_general(own_features, grad_proj, (((0,), (0,)), ((), ())), preferred_element_type=jnp.float32)
        return (running + weight_term, feature_grad)
    weight_sum, feature_grads = lax.scan(second_pass, jnp.zeros((H, H), jnp.float32), (grad_pres, edges_all, weights_all, node_blocks, sends, live_slots, returned, boundary.reshape(devices_all, B), owner_grad))
    weight_grad = weight_sum * (1.0 / math.sqrt(NODES))
    return (activated.reshape(NODES, H), feature_grads.reshape(NODES, H), weight_grad)
```

```python
import functools
import math

import jax
import jax.numpy as jnp
from jax import lax
from jax.experimental import pallas as pl
from jax.experimental.pallas import tpu as pltpu
from jax.sharding import PartitionSpec as P

BF16 = jnp.bfloat16
F32 = jnp.float32
BLOCK = 256
LANES = 128
MIB = 1 << 20
GELU_SCALE = math.sqrt(2.0 / math.pi)
GELU_CUBE = 0.044715


def contract(left, right, left_dim, right_dim):
    return lax.dot_general(
        left, right, (((left_dim,), (right_dim,)), ((), ())), preferred_element_type=F32
    )


def call(kernel, outs, *operands, **options):
    return pl.pallas_call(kernel, out_shape=outs, **options)(*operands)


def shape(dims, dtype):
    return jax.ShapeDtypeStruct(dims, dtype)


VMEM = pl.BlockSpec(memory_space=pltpu.VMEM)
SMEM = pl.BlockSpec(memory_space=pltpu.SMEM)
ANY = pl.BlockSpec(memory_space=pl.ANY)


def small_iota(dims, dim):
    return lax.broadcasted_iota(jnp.int32, dims, dim).astype(jnp.int16)


def one_hot(index, count):
    rows = index.shape[0]
    splat = jnp.broadcast_to(index, (rows, LANES)).astype(jnp.int16)
    lane = small_iota((rows, LANES), 1)
    tiles = []
    for tile in range(count // LANES):
        hit = splat == lane + jnp.int16(tile * LANES)
        tiles.append(jnp.where(hit, jnp.ones((), BF16), jnp.zeros((), BF16)))
    return jnp.concatenate(tiles, axis=1)


def gather_kernel(send_ref, counts_ref, bound_ref, feat_ref, out_ref, panel_ref):
    slots, peers = send_ref.shape
    nodes = feat_ref.shape[0]
    live = lax.broadcasted_iota(jnp.int32, (slots, peers), 0) < counts_ref[...]
    send = jnp.where(live, send_ref[...], -1)
    panel = bound_ref.shape[1]
    bound = jnp.transpose(jnp.broadcast_to(bound_ref[...], (panel, panel)))[:, :1]
    panel_ref[...] = jnp.dot(
        one_hot(bound, nodes), feat_ref[...], preferred_element_type=F32
    ).astype(BF16)
    group = BLOCK // slots
    for part in range(peers // group):
        index = jnp.concatenate(
            [send[:, peer : peer + 1] for peer in range(part * group, (part + 1) * group)], axis=0
        )
        out_ref[part * BLOCK : (part + 1) * BLOCK, :] = jnp.dot(
            one_hot(index, nodes), feat_ref[...], preferred_element_type=F32
        ).astype(BF16)


def build_kernel(
    own_blocks,
    index_ref,
    edge_weight_ref,
    feat_ref,
    weight_ref,
    cot_ref,
    cached_ref,
    mixer_ref,
    local_ref,
    cot_out_ref,
    cached_out_ref,
    index_rep,
    weight_rep,
    projected,
):
    step = pl.program_id(0)
    slots, nodes = index_ref.shape

    @pl.when(step == 0)
    def _():
        index = index_ref[...]
        merged = []
        for slot in range(slots):
            same = index == index[slot : slot + 1]
            merged.append(
                jnp.sum(jnp.where(same, edge_weight_ref[...], 0.0), axis=0, keepdims=True)
            )
        for slot in range(slots):
            index_rep[slot] = jnp.broadcast_to(index[slot : slot + 1], (16, nodes)).astype(
                jnp.int16
            )
            weight_rep[slot] = jnp.broadcast_to(merged[slot], (16, nodes)).astype(BF16)
        projected[...] = contract(weight_ref[...], feat_ref[...], 0, 1).astype(BF16)
        cot_out_ref[...] = jnp.transpose(cot_ref[...])
        cached_out_ref[...] = jnp.transpose(cached_ref[...])
        local_ref[...] = jnp.zeros_like(local_ref)

    def tile(number, carry):
        lanes = pl.ds(pl.multiple_of(number * LANES, LANES), LANES)
        index = [index_rep[slot, :, lanes] for slot in range(slots)]
        weights = [weight_rep[slot, :, lanes] for slot in range(slots)]
        row = (lax.broadcasted_iota(jnp.int32, (16, LANES), 0) + step * BLOCK).astype(jnp.int16)
        for sub in range(BLOCK // 16):
            here = row + jnp.int16(sub * 16)
            value = jnp.zeros((16, LANES), BF16)
            for slot in range(slots):
                value = jnp.where(index[slot] == here, weights[slot], value)
            mixer_ref[sub * 16 : sub * 16 + 16, lanes] = value
        return carry

    lax.fori_loop(0, nodes // LANES, tile, 0)

    @pl.when(step < own_blocks)
    def _():
        columns = pl.ds(pl.multiple_of(step * BLOCK, BLOCK), BLOCK)
        local_ref[...] += jnp.dot(
            projected[:, columns], mixer_ref[...], preferred_element_type=F32
        )


def middle_kernel(
    first_row,
    skip_ref,
    arrived_ref,
    fresh_ref,
    cached_ref,
    weight_ref,
    local_ref,
    cot_ref,
    mixer_ref,
    act_ref,
    grad_ref,
    remote_ref,
    panel_ref,
    mixer,
    table,
    sems,
):
    rows, nodes = mixer.shape
    groups = skip_ref.shape[0]
    remote = arrived_ref.shape[0]
    panel = fresh_ref.shape[0] // groups
    blocks = nodes // BLOCK

    def load(number):
        lanes = pl.ds(pl.multiple_of(number * BLOCK, BLOCK), BLOCK)
        return pltpu.make_async_copy(
            mixer_ref.at[pl.ds(first_row, rows), lanes], mixer.at[:, lanes], sems.at[number]
        )

    for number in range(blocks):
        load(number).start()
    for start in range(0, remote, 512):
        table[:, start : start + 512] = contract(
            weight_ref[...], arrived_ref[start : start + 512, :], 0, 1
        ).astype(BF16)
    for group in range(groups):
        fresh = contract(
            weight_ref[...], fresh_ref[group * panel : (group + 1) * panel, :], 0, 1
        ).astype(BF16)
        stale = cached_ref[:, group * panel : (group + 1) * panel]
        table[:, remote + group * panel : remote + (group + 1) * panel] = jnp.where(
            skip_ref[group] == 1, stale, fresh
        )

    def forward(number, carry):
        load(number).wait()
        lanes = pl.ds(pl.multiple_of(number * BLOCK, BLOCK), BLOCK)
        x = local_ref[:, lanes] + jnp.dot(
            table[...], mixer[:, lanes], preferred_element_type=F32
        )
        square = x * x
        bend = jnp.tanh(GELU_SCALE * x * (1.0 + GELU_CUBE * square))
        half = 0.5 * (1.0 + bend)
        act_ref[:, lanes] = (x * half).astype(BF16)
        slope = half + (0.5 * GELU_SCALE) * x * (1.0 - bend * bend) * (
            1.0 + (3.0 * GELU_CUBE) * square
        )
        grad_ref[:, lanes] = (cot_ref[:, lanes].astype(F32) * slope).astype(BF16)
        return carry

    lax.fori_loop(0, blocks, forward, 0)

    def backward(number, carry):
        start = pl.multiple_of(number * BLOCK, BLOCK)
        remote_ref[pl.ds(start, BLOCK), :] = contract(
            mixer[pl.ds(start, BLOCK), :], grad_ref[...], 1, 1
        ).astype(BF16)
        return carry

    lax.fori_loop(0, remote // BLOCK, backward, 0)
    for group in range(groups):
        start = remote + group * panel
        value = contract(mixer[start : start + panel, :], grad_ref[...], 1, 1)
        panel_ref[group * panel : (group + 1) * panel, :] = jnp.where(
            skip_ref[group] == 1, 0.0, value
        ).astype(BF16)


def local_kernel(
    mixer_ref,
    grad_ref,
    act_ref,
    feat_ref,
    arrived_ref,
    fresh_ref,
    remote_ref,
    panel_ref,
    grad_out_ref,
    term_ref,
    act_out_ref,
):
    step = pl.program_id(0)
    rows = pl.ds(pl.multiple_of(step * BLOCK, BLOCK), BLOCK)
    value = contract(mixer_ref[...], grad_ref[...], 1, 1)
    grad_out_ref[...] = value

    @pl.when(step == 0)
    def _():
        term_ref[...] = contract(arrived_ref[...], remote_ref[...], 0, 0) + contract(
            fresh_ref[...], panel_ref[...], 0, 0
        )

    term_ref[...] += contract(feat_ref[...], value.astype(BF16), 0, 0)
    act_out_ref[...] = jnp.transpose(act_ref[:, rows])


def final_kernel(
    send_ref, bound_ref, local_ref, returned_ref, owner_ref, weight_ref, out_ref, owner_pair
):
    step = pl.program_id(0)
    slots = send_ref.shape[1]
    panel = bound_ref.shape[1]

    @pl.when(step == 0)
    def _():
        total = jnp.sum(owner_ref[...].astype(F32), axis=0)
        high = total.astype(BF16)
        owner_pair[:panel] = high
        owner_pair[panel:] = (total - high.astype(F32)).astype(BF16)

    row = (lax.broadcasted_iota(jnp.int32, (BLOCK, LANES), 0) + step * BLOCK).astype(jnp.int16)

    def columns(ref, start):
        index = jnp.broadcast_to(ref[:, start : start + LANES], (BLOCK, LANES)).astype(jnp.int16)
        return jnp.where(index == row, jnp.ones((), BF16), jnp.zeros((), BF16))

    pick = jnp.concatenate(
        [columns(send_ref, start) for start in range(0, slots, LANES)], axis=1
    )
    pick_owner = jnp.concatenate(
        [columns(bound_ref, start) for start in range(0, panel, LANES)] * 2, axis=1
    )
    total = (
        local_ref[...]
        + jnp.dot(pick, returned_ref[...], preferred_element_type=F32)
        + jnp.dot(pick_owner, owner_pair[...], preferred_element_type=F32)
    )
    out_ref[...] = contract(total.astype(BF16), weight_ref[...], 1, 1).astype(BF16)


def shards(
    features,
    weight,
    cotangent,
    edge_index,
    edge_weight,
    send_rows,
    counts,
    boundary,
    skip_flags,
    cached_panels,
):
    nodes, width = features.shape
    peers = lax.axis_size("dom")
    groups = lax.axis_size("grp")
    fanout = edge_index.shape[1]
    slots = send_rows.shape[1]
    panel = boundary.shape[0]
    remote = peers * slots
    table = nodes + remote + groups * panel
    bound_row = boundary.reshape(1, panel)

    with jax.named_scope("gather_sent_rows"):
        outgoing, own_panel = call(
            gather_kernel,
            (shape((remote, width), BF16), shape((panel, width), BF16)),
            send_rows.T,
            counts.reshape(1, peers),
            bound_row,
            features,
            in_specs=[VMEM] * 4,
            out_specs=[VMEM] * 2,
            compiler_params=pltpu.CompilerParams(vmem_limit_bytes=24 * MIB),
        )
    arrived = lax.all_to_all(
        outgoing.reshape(peers, slots, width), "dom", split_axis=0, concat_axis=0, tiled=True
    ).reshape(remote, width)
    fresh = lax.all_gather(own_panel, "grp", axis=0, tiled=True)

    with jax.named_scope("build_mixer"):
        whole = lambda dims: pl.BlockSpec(dims, lambda step: (0,) * len(dims))
        mixer, local_pre, cot_t, cached_t = call(
            functools.partial(build_kernel, nodes // BLOCK),
            (
                shape((table, nodes), BF16),
                shape((width, nodes), F32),
                shape((width, nodes), BF16),
                shape((width, groups * panel), BF16),
            ),
            edge_index.T,
            edge_weight.T,
            features,
            weight,
            cotangent,
            cached_panels.reshape(groups * panel, width),
            grid=(table // BLOCK,),
            in_specs=[
                whole((fanout, nodes)),
                whole((fanout, nodes)),
                whole((nodes, width)),
                whole((width, width)),
                whole((nodes, width)),
                whole((groups * panel, width)),
            ],
            out_specs=[
                pl.BlockSpec((BLOCK, nodes), lambda step: (step, 0)),
                whole((width, nodes)),
                whole((width, nodes)),
                whole((width, groups * panel)),
            ],
            scratch_shapes=[
                pltpu.VMEM((fanout, 16, nodes), jnp.int16),
                pltpu.VMEM((fanout, 16, nodes), BF16),
                pltpu.VMEM((width, nodes), BF16),
            ],
            compiler_params=pltpu.CompilerParams(vmem_limit_bytes=30 * MIB),
            cost_estimate=pl.CostEstimate(
                flops=2 * nodes * nodes * width,
                bytes_accessed=2 * table * nodes,
                transcendentals=0,
            ),
        )

    others = table - nodes
    with jax.named_scope("forward_and_remote_grads"):
        act_t, grad_t, remote_grad, panel_grad = call(
            functools.partial(middle_kernel, nodes),
            (
                shape((width, nodes), BF16),
                shape((width, nodes), BF16),
                shape((remote, width), BF16),
                shape((groups * panel, width), BF16),
            ),
            skip_flags.reshape(groups),
            arrived,
            fresh,
            cached_t,
            weight,
            local_pre,
            cot_t,
            mixer,
            in_specs=[SMEM] + [VMEM] * 6 + [ANY],
            out_specs=[VMEM] * 4,
            scratch_shapes=[
                pltpu.VMEM((others, nodes), BF16),
                pltpu.VMEM((width, others), BF16),
                pltpu.SemaphoreType.DMA((nodes // BLOCK,)),
            ],
            compiler_params=pltpu.CompilerParams(vmem_limit_bytes=50 * MIB),
        )
    returned = lax.all_to_all(
        remote_grad.reshape(peers, slots, width), "dom", split_axis=0, concat_axis=0, tiled=True
    ).reshape(remote, width)
    owner_grad = lax.psum_scatter(
        panel_grad.reshape(groups, panel, width), "grp", scatter_dimension=0, tiled=True
    )

    with jax.named_scope("own_grads"):
        local_grad, term, activated = call(
            local_kernel,
            (shape((nodes, width), F32), shape((width, width), F32), shape((nodes, width), BF16)),
            mixer,
            grad_t,
            act_t,
            features,
            arrived,
            fresh,
            remote_grad,
            panel_grad,
            grid=(nodes // BLOCK,),
            in_specs=[
                pl.BlockSpec((BLOCK, nodes), lambda step: (step, 0)),
                whole((width, nodes)),
                whole((width, nodes)),
                pl.BlockSpec((BLOCK, width), lambda step: (step, 0)),
                whole((remote, width)),
                whole((groups * panel, width)),
                whole((remote, width)),
                whole((groups * panel, width)),
            ],
            out_specs=[
                pl.BlockSpec((BLOCK, width), lambda step: (step, 0)),
                whole((width, width)),
                pl.BlockSpec((BLOCK, width), lambda step: (step, 0)),
            ],
            compiler_params=pltpu.CompilerParams(vmem_limit_bytes=30 * MIB),
            cost_estimate=pl.CostEstimate(
                flops=2 * nodes * nodes * width + 2 * table * width * width,
                bytes_accessed=2 * nodes * nodes,
                transcendentals=0,
            ),
        )

    parts = lax.all_to_all(
        term.reshape(peers, width // peers, width), "dom", split_axis=0, concat_axis=0, tiled=True
    )
    part = jnp.sum(parts, axis=0)
    parts = lax.all_to_all(
        jnp.broadcast_to(part[None], (groups,) + part.shape),
        "grp",
        split_axis=0,
        concat_axis=0,
        tiled=True,
    )
    part = jnp.sum(parts, axis=0) * (1.0 / math.sqrt(nodes * peers * groups))
    weight_grad = lax.all_to_all(
        jnp.broadcast_to(part[None], (peers,) + part.shape),
        "dom",
        split_axis=0,
        concat_axis=0,
        tiled=True,
    ).reshape(width, width)

    live = lax.broadcasted_iota(jnp.int32, send_rows.shape, 1) < counts[:, None]
    send_row = jnp.where(live, send_rows, -1).reshape(1, remote)
    with jax.named_scope("add_returned_rows"):
        feature_grad = call(
            final_kernel,
            shape((nodes, width), BF16),
            send_row,
            bound_row,
            local_grad,
            returned,
            owner_grad,
            weight,
            grid=(nodes // BLOCK,),
            in_specs=[
                whole((1, remote)),
                whole((1, panel)),
                pl.BlockSpec((BLOCK, width), lambda step: (step, 0)),
                whole((remote, width)),
                whole(owner_grad.shape),
                whole((width, width)),
            ],
            out_specs=pl.BlockSpec((BLOCK, width), lambda step: (step, 0)),
            scratch_shapes=[pltpu.VMEM((2 * panel, width), BF16)],
            compiler_params=pltpu.CompilerParams(vmem_limit_bytes=24 * MIB),
        )
    return (activated, feature_grad, weight_grad)


def solution(mesh):
    in_specs = (
        P(("dom", "grp"), None),
        P(),
        P(("dom", "grp"), None),
        P(("dom", "grp"), None),
        P(("dom", "grp"), None),
        P(("dom", "grp"), None),
        P(("dom", "grp")),
        P(("dom", "grp")),
        P("dom", None),
        P("dom", None, None, None),
    )
    out_specs = (P(("dom", "grp"), None), P(("dom", "grp"), None), P())
    return jax.shard_map(shards, mesh=mesh, in_specs=in_specs, out_specs=out_specs, check_vma=False)
```

```python
import functools
import math

import jax
import jax.numpy as jnp
from jax import lax
from jax.experimental import pallas as pl
from jax.experimental.pallas import tpu as pltpu
from jax.sharding import PartitionSpec as P

BF16 = jnp.bfloat16
F32 = jnp.float32
BLOCK = 256
LANES = 128
MIB = 1 << 20
PANEL_ROWS = 176
GELU_SCALE = math.sqrt(2.0 / math.pi)
GELU_CUBE = 0.044715


def contract(left, right, left_dim, right_dim):
    return lax.dot_general(
        left, right, (((left_dim,), (right_dim,)), ((), ())), preferred_element_type=F32
    )


def call(kernel, outs, *operands, **options):
    return pl.pallas_call(kernel, out_shape=outs, **options)(*operands)


def shape(dims, dtype):
    return jax.ShapeDtypeStruct(dims, dtype)


VMEM = pl.BlockSpec(memory_space=pltpu.VMEM)
SMEM = pl.BlockSpec(memory_space=pltpu.SMEM)
ANY = pl.BlockSpec(memory_space=pl.ANY)


def small_iota(dims, dim):
    return lax.broadcasted_iota(jnp.int32, dims, dim).astype(jnp.int16)


def one_hot(index, count):
    rows = index.shape[0]
    splat = jnp.broadcast_to(index, (rows, LANES)).astype(jnp.int16)
    lane = small_iota((rows, LANES), 1)
    tiles = []
    for tile in range(count // LANES):
        hit = splat == lane + jnp.int16(tile * LANES)
        tiles.append(jnp.where(hit, jnp.ones((), BF16), jnp.zeros((), BF16)))
    return jnp.concatenate(tiles, axis=1)


def gather_kernel(send_ref, counts_ref, feat_ref, out_ref):
    slots, peers = send_ref.shape
    nodes = feat_ref.shape[0]
    live = lax.broadcasted_iota(jnp.int32, (slots, peers), 0) < counts_ref[...]
    send = jnp.where(live, send_ref[...], -1)
    group = 2 * BLOCK // slots
    for part in range(peers // group):
        index = jnp.concatenate(
            [send[:, peer : peer + 1] for peer in range(part * group, (part + 1) * group)], axis=0
        )
        out_ref[part * 2 * BLOCK : (part + 1) * 2 * BLOCK, :] = jnp.dot(
            one_hot(index, nodes), feat_ref[...], preferred_element_type=F32
        ).astype(BF16)


def panel_kernel(bound_ref, feat_ref, panel_ref):
    nodes = feat_ref.shape[0]
    panel = bound_ref.shape[1]
    bound = jnp.transpose(jnp.broadcast_to(bound_ref[...], (panel, panel)))[:, :1]
    panel_ref[:panel, :] = jnp.dot(
        one_hot(bound, nodes), feat_ref[...], preferred_element_type=F32
    ).astype(BF16)
    panel_ref[panel:, :] = jnp.zeros((panel_ref.shape[0] - panel, feat_ref.shape[1]), BF16)


def build_kernel(
    own_blocks,
    panel_blocks,
    skip_ref,
    index_ref,
    edge_weight_ref,
    feat_ref,
    cached_ref,
    mixer_ref,
    sum_ref,
    stale_ref,
    index_rep,
    weight_rep,
):
    step = pl.program_id(0)
    slots, nodes = index_ref.shape
    wide = 2 * LANES

    @pl.when(step == 0)
    def _():
        index = index_ref[...]
        for slot in range(slots):
            same = index == index[slot : slot + 1]
            merged = jnp.sum(jnp.where(same, edge_weight_ref[...], 0.0), axis=0, keepdims=True)
            index_rep[slot] = jnp.broadcast_to(index[slot : slot + 1], (16, nodes)).astype(
                jnp.int16
            )
            weight_rep[slot] = jnp.broadcast_to(merged, (16, nodes)).astype(BF16)
        sum_ref[...] = jnp.zeros_like(sum_ref)
        stale_ref[...] = jnp.zeros_like(stale_ref)

    row = (lax.broadcasted_iota(jnp.int32, (16, wide), 0) + step * BLOCK).astype(jnp.int16)

    def tile(number, carry):
        lanes = pl.ds(pl.multiple_of(number * wide, wide), wide)
        index = [index_rep[slot, :, lanes] for slot in range(slots)]
        weights = [weight_rep[slot, :, lanes] for slot in range(slots)]
        for start in range(0, BLOCK, 16):
            here = row + jnp.int16(start)
            value = jnp.zeros((16, wide), BF16)
            for slot in range(slots):
                value = jnp.where(index[slot] == here, weights[slot], value)
            mixer_ref[start : start + 16, lanes] = value
        return carry

    lax.fori_loop(0, nodes // wide, tile, 0)

    @pl.when(step < own_blocks)
    def _():
        rows = pl.ds(pl.multiple_of(step * BLOCK, BLOCK), BLOCK)
        sum_ref[...] += contract(mixer_ref[...], feat_ref[rows, :], 0, 0)

    @pl.when(step >= panel_blocks)
    def _():
        panel = cached_ref.shape[0] // skip_ref.shape[0]
        first = (step - panel_blocks) * (BLOCK // panel)
        pieces = []
        for part in range(BLOCK // panel):
            rows = pl.ds(pl.multiple_of((first + part) * panel, panel), panel)
            pieces.append(
                jnp.where(skip_ref[first + part] == 1, cached_ref[rows, :], jnp.zeros((), BF16))
            )
        stale_ref[...] += contract(mixer_ref[...], jnp.concatenate(pieces, axis=0), 0, 0)


def middle_kernel(
    first_row,
    skip_ref,
    arrived_ref,
    fresh_ref,
    weight_ref,
    sum_ref,
    stale_ref,
    cot_ref,
    mixer_ref,
    act_ref,
    grad_ref,
    back_ref,
    panel_ref,
    mixer,
    table,
    sems,
):
    rows, nodes = mixer.shape
    groups = skip_ref.shape[0]
    remote = arrived_ref.shape[0]
    panel = (rows - remote) // groups
    stride = fresh_ref.shape[0] // groups
    width = weight_ref.shape[0]
    peers, peer_rows, _ = back_ref.shape
    slots = remote // peers
    wide = 2 * BLOCK
    blocks = nodes // wide

    def load(number):
        lanes = pl.ds(number * wide, wide)
        return pltpu.make_async_copy(
            mixer_ref.at[pl.ds(first_row, rows), lanes], mixer.at[:, lanes], sems.at[number]
        )

    for number in range(blocks):
        load(number).start()
    table[:remote, :] = arrived_ref[...]
    for group in range(groups):
        table[remote + group * panel : remote + (group + 1) * panel, :] = jnp.where(
            skip_ref[group] == 1,
            jnp.zeros((), BF16),
            fresh_ref[group * stride : group * stride + panel, :],
        )

    term = jnp.zeros((width, width), F32)
    for number in range(blocks):
        load(number).wait()
        here = slice(number * wide, (number + 1) * wide)
        mixed = (sum_ref[here, :] + contract(mixer[:, here], table[...], 0, 0)).astype(BF16)
        x = stale_ref[here, :] + jnp.dot(mixed, weight_ref[...], preferred_element_type=F32)
        square = x * x
        bend = jnp.tanh(GELU_SCALE * x * (1.0 + GELU_CUBE * square))
        half = 0.5 * (1.0 + bend)
        act_ref[here, :] = (x * half).astype(BF16)
        slope = half + (0.5 * GELU_SCALE) * x * (1.0 - bend * bend) * (
            1.0 + (3.0 * GELU_CUBE) * square
        )
        grad = (cot_ref[here, :].astype(F32) * slope).astype(BF16)
        grad_ref[here, :] = grad
        term += contract(mixed, grad, 0, 0)

    high = term.astype(BF16)
    pair = jnp.concatenate([high, (term - high.astype(F32)).astype(BF16)], axis=0)
    share = width // peers
    place = lax.broadcasted_iota(jnp.int32, (2 * width, 2 * width), 0)
    source = lax.broadcasted_iota(jnp.int32, (2 * width, 2 * width), 1)
    peer, offset = place // (2 * share), place % (2 * share)
    wanted = jnp.where(
        offset < share, peer * share + offset, width + peer * share + offset - share
    )
    shares = jnp.dot(
        jnp.where(source == wanted, 1.0, 0.0).astype(BF16), pair, preferred_element_type=F32
    )
    for peer in range(peers):
        back_ref[peer, slots:, :] = shares[peer * 2 * share : (peer + 1) * 2 * share].astype(BF16)

    for start in range(0, remote, wide):
        value = jnp.dot(
            mixer[start : start + wide, :], grad_ref[...], preferred_element_type=F32
        ).astype(BF16)
        for part in range(wide // slots):
            back_ref[start // slots + part, :slots, :] = value[part * slots : (part + 1) * slots]
    for start in range(0, groups * panel, wide):
        value = jnp.dot(
            mixer[remote + start : remote + start + wide, :],
            grad_ref[...],
            preferred_element_type=F32,
        )
        for part in range(wide // panel):
            panel_ref[start + part * panel : start + (part + 1) * panel, :] = jnp.where(
                skip_ref[start // panel + part] == 1,
                0.0,
                value[part * panel : (part + 1) * panel],
            ).astype(BF16)


def local_kernel(mixer_ref, grad_ref, out_ref):
    out_ref[...] = jnp.dot(mixer_ref[...], grad_ref[...], preferred_element_type=F32)


def final_kernel(
    send_ref, bound_ref, local_ref, returned_ref, owner_ref, weight_ref, out_ref, owner_pair
):
    step = pl.program_id(0)
    slots = send_ref.shape[1]
    panel = bound_ref.shape[1]

    @pl.when(step == 0)
    def _():
        total = jnp.sum(owner_ref[...].astype(F32), axis=0)
        high = total.astype(BF16)
        owner_pair[:panel] = high
        owner_pair[panel:] = (total - high.astype(F32)).astype(BF16)

    row = (lax.broadcasted_iota(jnp.int32, (BLOCK, LANES), 0) + step * BLOCK).astype(jnp.int16)

    def columns(ref, start):
        index = jnp.broadcast_to(ref[:, start : start + LANES], (BLOCK, LANES)).astype(jnp.int16)
        return jnp.where(index == row, jnp.ones((), BF16), jnp.zeros((), BF16))

    pick = jnp.concatenate(
        [columns(send_ref, start) for start in range(0, slots, LANES)], axis=1
    )
    pick_owner = jnp.concatenate(
        [columns(bound_ref, start) for start in range(0, panel, LANES)] * 2, axis=1
    )
    total = (
        local_ref[...]
        + jnp.dot(pick, returned_ref[...], preferred_element_type=F32)
        + jnp.dot(pick_owner, owner_pair[...], preferred_element_type=F32)
    )
    out_ref[...] = contract(total.astype(BF16), weight_ref[...], 1, 1).astype(BF16)


def whole(dims):
    return pl.BlockSpec(dims, lambda step: (0,) * len(dims))


def vmem(mib):
    return pltpu.CompilerParams(vmem_limit_bytes=mib * MIB)


def gather_sent(send_rows, counts, features):
    peers, slots = send_rows.shape
    with jax.named_scope("gather_sent_rows"):
        return call(
            gather_kernel,
            shape((peers * slots, features.shape[1]), BF16),
            send_rows.T,
            counts.reshape(1, peers),
            features,
            in_specs=[VMEM] * 3,
            out_specs=VMEM,
            compiler_params=vmem(16),
        )


def gather_panel(bound_row, features, rows):
    with jax.named_scope("gather_panel"):
        return call(
            panel_kernel,
            shape((rows, features.shape[1]), BF16),
            bound_row,
            features,
            in_specs=[VMEM] * 2,
            out_specs=VMEM,
            compiler_params=vmem(8),
        )


def build(skip, edge_index, edge_weight, features, cached, table):
    nodes, width = features.shape
    fanout = edge_index.shape[1]
    with jax.named_scope("build_mixer"):
        return call(
            functools.partial(build_kernel, nodes // BLOCK, (table - cached.shape[0]) // BLOCK),
            (
                shape((table, nodes), BF16),
                shape((nodes, width), F32),
                shape((nodes, width), F32),
            ),
            skip,
            edge_index.T,
            edge_weight.T,
            features,
            cached,
            grid=(table // BLOCK,),
            in_specs=[
                SMEM,
                whole((fanout, nodes)),
                whole((fanout, nodes)),
                whole((nodes, width)),
                whole(cached.shape),
            ],
            out_specs=[
                pl.BlockSpec((BLOCK, nodes), lambda step: (step, 0)),
                whole((nodes, width)),
                whole((nodes, width)),
            ],
            scratch_shapes=[
                pltpu.VMEM((fanout, 16, nodes), jnp.int16),
                pltpu.VMEM((fanout, 16, nodes), BF16),
            ],
            compiler_params=vmem(44),
            cost_estimate=pl.CostEstimate(
                flops=4 * nodes * nodes * width,
                bytes_accessed=2 * table * nodes,
                transcendentals=0,
            ),
        )


def middle(skip, arrived, fresh, weight, own_sum, stale, cotangent, mixer, peers, panel_rows):
    nodes, width = own_sum.shape
    remote = arrived.shape[0]
    others = mixer.shape[0] - nodes
    with jax.named_scope("forward_and_remote_grads"):
        return call(
            functools.partial(middle_kernel, nodes),
            (
                shape((nodes, width), BF16),
                shape((nodes, width), BF16),
                shape((peers, remote // peers + 2 * width // peers, width), BF16),
                shape((panel_rows, width), BF16),
            ),
            skip,
            arrived,
            fresh,
            weight,
            own_sum,
            stale,
            cotangent,
            mixer,
            in_specs=[SMEM] + [VMEM] * 6 + [ANY],
            out_specs=[VMEM] * 4,
            scratch_shapes=[
                pltpu.VMEM((others, nodes), BF16),
                pltpu.VMEM((others, width), BF16),
                pltpu.SemaphoreType.DMA((nodes // (2 * BLOCK),)),
            ],
            compiler_params=vmem(32),
        )


def own_grads(mixer, grad_pre):
    nodes, width = grad_pre.shape
    with jax.named_scope("own_grads"):
        return call(
            local_kernel,
            shape((nodes, width), F32),
            mixer,
            grad_pre,
            grid=(nodes // (2 * BLOCK),),
            in_specs=[
                pl.BlockSpec((2 * BLOCK, nodes), lambda step: (step, 0)),
                whole((nodes, width)),
            ],
            out_specs=pl.BlockSpec((2 * BLOCK, width), lambda step: (step, 0)),
            compiler_params=vmem(44),
            cost_estimate=pl.CostEstimate(
                flops=2 * nodes * nodes * width, bytes_accessed=2 * nodes * nodes, transcendentals=0
            ),
        )


def finish(send_row, bound_row, local_grad, returned, owner_grad, weight):
    nodes, width = local_grad.shape
    panel = bound_row.shape[1]
    with jax.named_scope("add_returned_rows"):
        return call(
            final_kernel,
            shape((nodes, width), BF16),
            send_row,
            bound_row,
            local_grad,
            returned,
            owner_grad,
            weight,
            grid=(nodes // BLOCK,),
            in_specs=[
                whole(send_row.shape),
                whole((1, panel)),
                pl.BlockSpec((BLOCK, width), lambda step: (step, 0)),
                whole(returned.shape),
                whole(owner_grad.shape),
                whole((width, width)),
            ],
            out_specs=pl.BlockSpec((BLOCK, width), lambda step: (step, 0)),
            scratch_shapes=[pltpu.VMEM((2 * panel, width), BF16)],
            compiler_params=vmem(16),
        )


def exchange(values, axis):
    return lax.all_to_all(values, axis, split_axis=0, concat_axis=0, tiled=True)


def everyone(part, axis):
    return exchange(jnp.broadcast_to(part[None], (lax.axis_size(axis),) + part.shape), axis)


def shards(
    features,
    weight,
    cotangent,
    edge_index,
    edge_weight,
    send_rows,
    counts,
    boundary,
    skip_flags,
    cached_panels,
):
    nodes, width = features.shape
    peers = lax.axis_size("dom")
    groups = lax.axis_size("grp")
    slots = send_rows.shape[1]
    panel = boundary.shape[0]
    remote = peers * slots
    table = nodes + remote + groups * panel
    bound_row = boundary.reshape(1, panel)
    skip = skip_flags.reshape(groups)

    own_panel = gather_panel(bound_row, features, PANEL_ROWS)
    fresh = lax.all_gather(own_panel, "grp", axis=0, tiled=True)
    outgoing = gather_sent(send_rows, counts, features)
    arrived = exchange(outgoing.reshape(peers, slots, width), "dom").reshape(remote, width)
    mixer, own_sum, stale = build(
        skip,
        edge_index,
        edge_weight,
        features,
        cached_panels.reshape(groups * panel, width),
        table,
    )
    activated, grad_pre, back, panel_grad = middle(
        skip, arrived, fresh, weight, own_sum, stale, cotangent, mixer, peers, groups * panel
    )
    owner_grad = lax.psum_scatter(
        panel_grad.reshape(groups, panel, width), "grp", scatter_dimension=0, tiled=True
    )
    returned = exchange(back, "dom")
    local_grad = own_grads(mixer, grad_pre)
    returned, local_grad = lax.optimization_barrier((returned, local_grad))

    share = width // peers
    pairs = returned[:, slots:, :].astype(F32)
    part = jnp.sum(pairs[:, :share] + pairs[:, share:], axis=0)
    part = jnp.sum(everyone(part, "grp"), axis=0) * (1.0 / math.sqrt(nodes * peers * groups))
    weight_grad = everyone(part, "dom").reshape(width, width)

    live = lax.broadcasted_iota(jnp.int32, send_rows.shape, 1) < counts[:, None]
    send_row = jnp.pad(
        jnp.where(live, send_rows, -1), ((0, 0), (0, 2 * share)), constant_values=-1
    ).reshape(1, peers * (slots + 2 * share))
    feature_grad = finish(
        send_row, bound_row, local_grad, returned.reshape(-1, width), owner_grad, weight
    )
    return (activated, feature_grad, weight_grad)


def solution(mesh):
    in_specs = (
        P(("dom", "grp"), None),
        P(),
        P(("dom", "grp"), None),
        P(("dom", "grp"), None),
        P(("dom", "grp"), None),
        P(("dom", "grp"), None),
        P(("dom", "grp")),
        P(("dom", "grp")),
        P("dom", None),
        P("dom", None, None, None),
    )
    out_specs = (P(("dom", "grp"), None), P(("dom", "grp"), None), P())
    return jax.shard_map(shards, mesh=mesh, in_specs=in_specs, out_specs=out_specs, check_vma=False)
```

```python
import functools
import math

import jax
import jax.numpy as jnp
from jax import lax
from jax.experimental import pallas as pl
from jax.experimental.pallas import tpu as pltpu
from jax.sharding import PartitionSpec as P

BF16 = jnp.bfloat16
F32 = jnp.float32
BLOCK = 256
LANES = 128
MIB = 1 << 20
GELU_SCALE = math.sqrt(2.0 / math.pi)
GELU_CUBE = 0.044715


def contract(left, right, left_dim, right_dim):
    return lax.dot_general(
        left, right, (((left_dim,), (right_dim,)), ((), ())), preferred_element_type=F32
    )


def call(kernel, outs, *operands, **options):
    return pl.pallas_call(kernel, out_shape=outs, **options)(*operands)


def shape(dims, dtype):
    return jax.ShapeDtypeStruct(dims, dtype)


VMEM = pl.BlockSpec(memory_space=pltpu.VMEM)
SMEM = pl.BlockSpec(memory_space=pltpu.SMEM)
ANY = pl.BlockSpec(memory_space=pl.ANY)


def small_iota(dims, dim):
    return lax.broadcasted_iota(jnp.int32, dims, dim).astype(jnp.int16)


def one_hot(index, count):
    rows = index.shape[0]
    splat = jnp.broadcast_to(index, (rows, LANES)).astype(jnp.int16)
    lane = small_iota((rows, LANES), 1)
    tiles = []
    for tile in range(count // LANES):
        hit = splat == lane + jnp.int16(tile * LANES)
        tiles.append(jnp.where(hit, jnp.ones((), BF16), jnp.zeros((), BF16)))
    return jnp.concatenate(tiles, axis=1)


def gather_kernel(send_ref, counts_ref, feat_ref, out_ref):
    slots, peers = send_ref.shape
    nodes = feat_ref.shape[0]
    live = lax.broadcasted_iota(jnp.int32, (slots, peers), 0) < counts_ref[...]
    send = jnp.where(live, send_ref[...], -1)
    group = 2 * BLOCK // slots
    for part in range(peers // group):
        index = jnp.concatenate(
            [send[:, peer : peer + 1] for peer in range(part * group, (part + 1) * group)], axis=0
        )
        out_ref[part * 2 * BLOCK : (part + 1) * 2 * BLOCK, :] = jnp.dot(
            one_hot(index, nodes), feat_ref[...], preferred_element_type=F32
        ).astype(BF16)


def panel_kernel(bound_ref, feat_ref, panel_ref):
    nodes = feat_ref.shape[0]
    panel = bound_ref.shape[1]
    bound = jnp.transpose(jnp.broadcast_to(bound_ref[...], (panel, panel)))[:, :1]
    panel_ref[...] = jnp.dot(
        one_hot(bound, nodes), feat_ref[...], preferred_element_type=F32
    ).astype(BF16)


def build_kernel(
    own_blocks,
    panel_blocks,
    skip_ref,
    index_ref,
    edge_weight_ref,
    feat_ref,
    cached_ref,
    mixer_ref,
    sum_ref,
    stale_ref,
    index_rep,
    weight_rep,
):
    step = pl.program_id(0)
    slots, nodes = index_ref.shape
    wide = 2 * LANES

    @pl.when(step == 0)
    def _():
        index = index_ref[...]
        for slot in range(slots):
            same = index == index[slot : slot + 1]
            merged = jnp.sum(jnp.where(same, edge_weight_ref[...], 0.0), axis=0, keepdims=True)
            index_rep[slot] = jnp.broadcast_to(index[slot : slot + 1], (16, nodes)).astype(
                jnp.int16
            )
            weight_rep[slot] = jnp.broadcast_to(merged, (16, nodes)).astype(BF16)
        sum_ref[...] = jnp.zeros_like(sum_ref)
        stale_ref[...] = jnp.zeros_like(stale_ref)

    row = (lax.broadcasted_iota(jnp.int32, (16, wide), 0) + step * BLOCK).astype(jnp.int16)

    def tile(number, carry):
        lanes = pl.ds(pl.multiple_of(number * wide, wide), wide)
        index = [index_rep[slot, :, lanes] for slot in range(slots)]
        weights = [weight_rep[slot, :, lanes] for slot in range(slots)]
        for start in range(0, BLOCK, 16):
            here = row + jnp.int16(start)
            value = jnp.zeros((16, wide), BF16)
            for slot in range(slots):
                value = jnp.where(index[slot] == here, weights[slot], value)
            mixer_ref[start : start + 16, lanes] = value
        return carry

    lax.fori_loop(0, nodes // wide, tile, 0)

    @pl.when(step < own_blocks)
    def _():
        rows = pl.ds(pl.multiple_of(step * BLOCK, BLOCK), BLOCK)
        sum_ref[...] += contract(mixer_ref[...], feat_ref[rows, :], 0, 0)

    @pl.when(step >= panel_blocks)
    def _():
        panel = cached_ref.shape[0] // skip_ref.shape[0]
        first = (step - panel_blocks) * (BLOCK // panel)
        pieces = []
        for part in range(BLOCK // panel):
            rows = pl.ds(pl.multiple_of((first + part) * panel, panel), panel)
            pieces.append(
                jnp.where(skip_ref[first + part] == 1, cached_ref[rows, :], jnp.zeros((), BF16))
            )
        stale_ref[...] += contract(mixer_ref[...], jnp.concatenate(pieces, axis=0), 0, 0)


def middle_kernel(
    first_row,
    skip_ref,
    weight_ref,
    arrived_ref,
    fresh_ref,
    sum_ref,
    stale_ref,
    cot_ref,
    mixer_ref,
    act_ref,
    grad_ref,
    back_ref,
    panel_ref,
    mixer,
    table,
    own_sum,
    stale,
    cot,
    act,
    grad,
    back,
    panel_back,
    in_sems,
    block_sems,
    out_sems,
):
    rows, nodes = mixer.shape
    groups = skip_ref.shape[0]
    remote, width = arrived_ref.shape
    panel = (rows - remote) // groups
    peers, peer_rows, _ = back.shape
    slots = remote // peers
    wide = 2 * BLOCK
    blocks = nodes // wide

    def load(number):
        lanes = pl.ds(number * wide, wide)
        return pltpu.make_async_copy(
            mixer_ref.at[pl.ds(first_row, rows), lanes], mixer.at[:, lanes], block_sems.at[number]
        )

    fetches = [
        pltpu.make_async_copy(source, target, in_sems.at[number])
        for number, (source, target) in enumerate(
            (
                (arrived_ref, table.at[pl.ds(0, remote)]),
                (fresh_ref, table.at[pl.ds(remote, groups * panel)]),
                (sum_ref, own_sum),
                (stale_ref, stale),
                (cot_ref, cot),
            )
        )
    ]
    for fetch in fetches[:2]:
        fetch.start()
    load(0).start()
    for fetch in fetches[2:]:
        fetch.start()
    for number in range(1, blocks):
        load(number).start()
    for fetch in fetches[:2]:
        fetch.wait()
    for group in range(groups):
        here = slice(remote + group * panel, remote + (group + 1) * panel)
        table[here, :] = jnp.where(skip_ref[group] == 1, jnp.zeros((), BF16), table[here, :])

    term = jnp.zeros((width, width), F32)
    for number in range(blocks):
        load(number).wait()
        here = slice(number * wide, (number + 1) * wide)
        product = contract(mixer[:, here], table[...], 0, 0)
        if number == 0:
            for fetch in fetches[2:]:
                fetch.wait()
        mixed = (own_sum[here, :] + product).astype(BF16)
        x = stale[here, :] + jnp.dot(mixed, weight_ref[...], preferred_element_type=F32)
        square = x * x
        bend = jnp.tanh(GELU_SCALE * x * (1.0 + GELU_CUBE * square))
        half = 0.5 * (1.0 + bend)
        act[here, :] = (x * half).astype(BF16)
        slope = half + (0.5 * GELU_SCALE) * x * (1.0 - bend * bend) * (
            1.0 + (3.0 * GELU_CUBE) * square
        )
        part = (cot[here, :].astype(F32) * slope).astype(BF16)
        grad[here, :] = part
        term += contract(mixed, part, 0, 0)

    out_copies = [
        pltpu.make_async_copy(act, act_ref, out_sems.at[0]),
        pltpu.make_async_copy(grad, grad_ref, out_sems.at[1]),
    ]
    for copy in out_copies:
        copy.start()

    high = term.astype(BF16)
    low = (term - high.astype(F32)).astype(BF16)
    across = width // LANES
    tall = width * across // peers
    for peer in range(peers):
        place = (
            slice(peer // across * tall, (peer // across + 1) * tall),
            slice(peer % across * LANES, (peer % across + 1) * LANES),
        )
        back[peer, slots:, :LANES] = high[place]
        back[peer, slots:, LANES:] = low[place]

    tall_block = remote // 2
    for start in range(0, remote, tall_block):
        value = jnp.dot(
            mixer[start : start + tall_block, :], grad[...], preferred_element_type=F32
        ).astype(BF16)
        first = start // slots
        count = tall_block // slots
        for part in range(count):
            back[first + part, :slots, :] = value[part * slots : (part + 1) * slots]
        copy = pltpu.make_async_copy(
            back.at[pl.ds(first, count)],
            back_ref.at[pl.ds(first, count)],
            out_sems.at[2 + start // tall_block],
        )
        copy.start()
        out_copies.append(copy)
    tall_block = groups * panel // 2
    for start in range(0, groups * panel, tall_block):
        value = jnp.dot(
            mixer[remote + start : remote + start + tall_block, :],
            grad[...],
            preferred_element_type=F32,
        )
        for part in range(tall_block // panel):
            panel_back[start + part * panel : start + (part + 1) * panel, :] = jnp.where(
                skip_ref[start // panel + part] == 1,
                0.0,
                value[part * panel : (part + 1) * panel],
            ).astype(BF16)
    copy = pltpu.make_async_copy(panel_back, panel_ref, out_sems.at[4])
    copy.start()
    for copy in out_copies + [copy]:
        copy.wait()


def local_kernel(mixer_ref, grad_ref, out_ref):
    out_ref[...] = jnp.dot(mixer_ref[...], grad_ref[...], preferred_element_type=F32)


def final_kernel(
    send_ref, bound_ref, local_ref, returned_ref, owner_ref, weight_ref, out_ref, owner_pair
):
    step = pl.program_id(0)
    slots = send_ref.shape[1]
    panel = bound_ref.shape[1]

    @pl.when(step == 0)
    def _():
        total = jnp.sum(owner_ref[...].astype(F32), axis=0)
        high = total.astype(BF16)
        owner_pair[:panel] = high
        owner_pair[panel:] = (total - high.astype(F32)).astype(BF16)

    row = (lax.broadcasted_iota(jnp.int32, (BLOCK, LANES), 0) + step * BLOCK).astype(jnp.int16)

    def columns(ref, start):
        index = jnp.broadcast_to(ref[:, start : start + LANES], (BLOCK, LANES)).astype(jnp.int16)
        return jnp.where(index == row, jnp.ones((), BF16), jnp.zeros((), BF16))

    pick = jnp.concatenate(
        [columns(send_ref, start) for start in range(0, slots, LANES)], axis=1
    )
    pick_owner = jnp.concatenate(
        [columns(bound_ref, start) for start in range(0, panel, LANES)] * 2, axis=1
    )
    total = (
        local_ref[...]
        + jnp.dot(pick, returned_ref[...], preferred_element_type=F32)
        + jnp.dot(pick_owner, owner_pair[...], preferred_element_type=F32)
    )
    out_ref[...] = contract(total.astype(BF16), weight_ref[...], 1, 1).astype(BF16)


def whole(dims):
    return pl.BlockSpec(dims, lambda step: (0,) * len(dims))


def vmem(mib):
    return pltpu.CompilerParams(vmem_limit_bytes=mib * MIB)


def gather_sent(send_rows, counts, features):
    peers, slots = send_rows.shape
    with jax.named_scope("gather_sent_rows"):
        return call(
            gather_kernel,
            shape((peers * slots, features.shape[1]), BF16),
            send_rows.T,
            counts.reshape(1, peers),
            features,
            in_specs=[VMEM] * 3,
            out_specs=VMEM,
            compiler_params=vmem(16),
        )


def gather_panel(bound_row, features):
    with jax.named_scope("gather_panel"):
        return call(
            panel_kernel,
            shape((bound_row.shape[1], features.shape[1]), BF16),
            bound_row,
            features,
            in_specs=[VMEM] * 2,
            out_specs=VMEM,
            compiler_params=vmem(8),
        )


def build(skip, edge_index, edge_weight, features, cached, table):
    nodes, width = features.shape
    fanout = edge_index.shape[1]
    with jax.named_scope("build_mixer"):
        return call(
            functools.partial(build_kernel, nodes // BLOCK, (table - cached.shape[0]) // BLOCK),
            (
                shape((table, nodes), BF16),
                shape((nodes, width), F32),
                shape((nodes, width), F32),
            ),
            skip,
            edge_index.T,
            edge_weight.T,
            features,
            cached,
            grid=(table // BLOCK,),
            in_specs=[
                SMEM,
                whole((fanout, nodes)),
                whole((fanout, nodes)),
                whole((nodes, width)),
                whole(cached.shape),
            ],
            out_specs=[
                pl.BlockSpec((BLOCK, nodes), lambda step: (step, 0)),
                whole((nodes, width)),
                whole((nodes, width)),
            ],
            scratch_shapes=[
                pltpu.VMEM((fanout, 16, nodes), jnp.int16),
                pltpu.VMEM((fanout, 16, nodes), BF16),
            ],
            compiler_params=vmem(44),
            cost_estimate=pl.CostEstimate(
                flops=4 * nodes * nodes * width,
                bytes_accessed=2 * table * nodes,
                transcendentals=0,
            ),
        )


def middle(skip, arrived, fresh, weight, own_sum, stale, cotangent, mixer, peers, panel_rows):
    nodes, width = own_sum.shape
    remote = arrived.shape[0]
    others = mixer.shape[0] - nodes
    back = (peers, remote // peers + width * width // (peers * LANES), width)
    with jax.named_scope("forward_and_remote_grads"):
        return call(
            functools.partial(middle_kernel, nodes),
            (
                shape((nodes, width), BF16),
                shape((nodes, width), BF16),
                shape(back, BF16),
                shape((panel_rows, width), BF16),
            ),
            skip,
            weight,
            arrived,
            fresh,
            own_sum,
            stale,
            cotangent,
            mixer,
            in_specs=[SMEM, VMEM] + [ANY] * 6,
            out_specs=[ANY] * 4,
            scratch_shapes=[
                pltpu.VMEM((others, nodes), BF16),
                pltpu.VMEM((others, width), BF16),
                pltpu.VMEM((nodes, width), F32),
                pltpu.VMEM((nodes, width), F32),
                pltpu.VMEM((nodes, width), BF16),
                pltpu.VMEM((nodes, width), BF16),
                pltpu.VMEM((nodes, width), BF16),
                pltpu.VMEM(back, BF16),
                pltpu.VMEM((panel_rows, width), BF16),
                pltpu.SemaphoreType.DMA((5,)),
                pltpu.SemaphoreType.DMA((nodes // (2 * BLOCK),)),
                pltpu.SemaphoreType.DMA((5,)),
            ],
            compiler_params=vmem(56),
        )


def own_grads(mixer, grad_pre):
    nodes, width = grad_pre.shape
    with jax.named_scope("own_grads"):
        return call(
            local_kernel,
            shape((nodes, width), F32),
            mixer,
            grad_pre,
            grid=(nodes // (2 * BLOCK),),
            in_specs=[
                pl.BlockSpec((2 * BLOCK, nodes), lambda step: (step, 0)),
                whole((nodes, width)),
            ],
            out_specs=pl.BlockSpec((2 * BLOCK, width), lambda step: (step, 0)),
            compiler_params=vmem(44),
            cost_estimate=pl.CostEstimate(
                flops=2 * nodes * nodes * width, bytes_accessed=2 * nodes * nodes, transcendentals=0
            ),
        )


def finish(send_row, bound_row, local_grad, returned, owner_grad, weight):
    nodes, width = local_grad.shape
    panel = bound_row.shape[1]
    with jax.named_scope("add_returned_rows"):
        return call(
            final_kernel,
            shape((nodes, width), BF16),
            send_row,
            bound_row,
            local_grad,
            returned,
            owner_grad,
            weight,
            grid=(nodes // BLOCK,),
            in_specs=[
                whole(send_row.shape),
                whole((1, panel)),
                pl.BlockSpec((BLOCK, width), lambda step: (step, 0)),
                whole(returned.shape),
                whole(owner_grad.shape),
                whole((width, width)),
            ],
            out_specs=pl.BlockSpec((BLOCK, width), lambda step: (step, 0)),
            scratch_shapes=[pltpu.VMEM((2 * panel, width), BF16)],
            compiler_params=vmem(16),
        )


def exchange(values, axis):
    return lax.all_to_all(values, axis, split_axis=0, concat_axis=0, tiled=True)


def everyone(part, axis):
    return exchange(jnp.broadcast_to(part[None], (lax.axis_size(axis),) + part.shape), axis)


def shards(
    features,
    weight,
    cotangent,
    edge_index,
    edge_weight,
    send_rows,
    counts,
    boundary,
    skip_flags,
    cached_panels,
):
    nodes, width = features.shape
    peers = lax.axis_size("dom")
    groups = lax.axis_size("grp")
    slots = send_rows.shape[1]
    panel = boundary.shape[0]
    remote = peers * slots
    table = nodes + remote + groups * panel
    bound_row = boundary.reshape(1, panel)
    skip = skip_flags.reshape(groups)

    own_panel = gather_panel(bound_row, features)
    fresh = lax.all_gather(own_panel, "grp", axis=0, tiled=True)
    skip, fresh = lax.optimization_barrier((skip, fresh))
    outgoing = gather_sent(send_rows, counts, features)
    arrived = exchange(outgoing.reshape(peers, slots, width), "dom").reshape(remote, width)
    mixer, own_sum, stale = build(
        skip,
        edge_index,
        edge_weight,
        features,
        cached_panels.reshape(groups * panel, width),
        table,
    )
    activated, grad_pre, back, panel_grad = middle(
        skip, arrived, fresh, weight, own_sum, stale, cotangent, mixer, peers, groups * panel
    )
    owner_grad = lax.psum_scatter(
        panel_grad.reshape(groups, panel, width), "grp", scatter_dimension=0, tiled=True
    )
    returned = exchange(back, "dom")
    local_grad = own_grads(mixer, grad_pre)
    returned, local_grad = lax.optimization_barrier((returned, local_grad))

    pairs = returned[:, slots:, :].astype(F32)
    part = jnp.sum(pairs[:, :, :LANES] + pairs[:, :, LANES:], axis=0)
    part = jnp.sum(everyone(part, "grp"), axis=0) * (1.0 / math.sqrt(nodes * peers * groups))
    across = width // LANES
    tall = part.shape[0]
    weight_grad = (
        everyone(part, "dom")
        .reshape(peers // across, across, tall, LANES)
        .transpose(0, 2, 1, 3)
        .reshape(width, width)
    )

    live = lax.broadcasted_iota(jnp.int32, send_rows.shape, 1) < counts[:, None]
    send_row = jnp.pad(
        jnp.where(live, send_rows, -1), ((0, 0), (0, tall)), constant_values=-1
    ).reshape(1, peers * (slots + tall))
    feature_grad = finish(
        send_row, bound_row, local_grad, returned.reshape(-1, width), owner_grad, weight
    )
    return (activated, feature_grad, weight_grad)


def solution(mesh):
    in_specs = (
        P(("dom", "grp"), None),
        P(),
        P(("dom", "grp"), None),
        P(("dom", "grp"), None),
        P(("dom", "grp"), None),
        P(("dom", "grp"), None),
        P(("dom", "grp")),
        P(("dom", "grp")),
        P("dom", None),
        P("dom", None, None, None),
    )
    out_specs = (P(("dom", "grp"), None), P(("dom", "grp"), None), P())
    return jax.shard_map(shards, mesh=mesh, in_specs=in_specs, out_specs=out_specs, check_vma=False)
```

```python
import functools
import math

import jax
import jax.numpy as jnp
from jax import lax
from jax.experimental import pallas as pl
from jax.experimental.pallas import tpu as pltpu
from jax.sharding import PartitionSpec as P

BF16 = jnp.bfloat16
F32 = jnp.float32
BLOCK = 256
BUILD_BLOCK = 512
LANES = 128
MIB = 1 << 20
GELU_SCALE = math.sqrt(2.0 / math.pi)
GELU_CUBE = 0.044715


def contract(left, right, left_dim, right_dim):
    return lax.dot_general(
        left, right, (((left_dim,), (right_dim,)), ((), ())), preferred_element_type=F32
    )


def call(kernel, outs, *operands, **options):
    return pl.pallas_call(kernel, out_shape=outs, **options)(*operands)


def shape(dims, dtype):
    return jax.ShapeDtypeStruct(dims, dtype)


VMEM = pl.BlockSpec(memory_space=pltpu.VMEM)
SMEM = pl.BlockSpec(memory_space=pltpu.SMEM)
ANY = pl.BlockSpec(memory_space=pl.ANY)


def small_iota(dims, dim):
    return lax.broadcasted_iota(jnp.int32, dims, dim).astype(jnp.int16)


def one_hot(index, count):
    rows = index.shape[0]
    splat = jnp.broadcast_to(index, (rows, LANES)).astype(jnp.int16)
    lane = small_iota((rows, LANES), 1)
    tiles = []
    for tile in range(count // LANES):
        hit = splat == lane + jnp.int16(tile * LANES)
        tiles.append(jnp.where(hit, jnp.ones((), BF16), jnp.zeros((), BF16)))
    return jnp.concatenate(tiles, axis=1)


def gather_kernel(send_ref, counts_ref, feat_ref, out_ref):
    slots, peers = send_ref.shape
    nodes = feat_ref.shape[0]
    live = lax.broadcasted_iota(jnp.int32, (slots, peers), 0) < counts_ref[...]
    send = jnp.where(live, send_ref[...], -1)
    group = 2 * BLOCK // slots
    for part in range(peers // group):
        index = jnp.concatenate(
            [send[:, peer : peer + 1] for peer in range(part * group, (part + 1) * group)], axis=0
        )
        out_ref[part * 2 * BLOCK : (part + 1) * 2 * BLOCK, :] = jnp.dot(
            one_hot(index, nodes), feat_ref[...], preferred_element_type=F32
        ).astype(BF16)


def panel_kernel(bound_ref, feat_ref, panel_ref):
    nodes = feat_ref.shape[0]
    panel = bound_ref.shape[1]
    bound = jnp.transpose(jnp.broadcast_to(bound_ref[...], (panel, panel)))[:, :1]
    panel_ref[...] = jnp.dot(
        one_hot(bound, nodes), feat_ref[...], preferred_element_type=F32
    ).astype(BF16)


def build_kernel(
    own_blocks,
    panel_blocks,
    skip_ref,
    index_ref,
    edge_weight_ref,
    feat_ref,
    cached_ref,
    mixer_ref,
    sum_ref,
    stale_ref,
    index_rep,
    weight_rep,
):
    step = pl.program_id(0)
    slots, nodes = index_ref.shape
    wide = 2 * LANES

    @pl.when(step == 0)
    def _():
        index = index_ref[...]
        for slot in range(slots):
            same = index == index[slot : slot + 1]
            merged = jnp.sum(jnp.where(same, edge_weight_ref[...], 0.0), axis=0, keepdims=True)
            index_rep[slot] = jnp.broadcast_to(index[slot : slot + 1], (16, nodes)).astype(
                jnp.int16
            )
            weight_rep[slot] = jnp.broadcast_to(merged, (16, nodes)).astype(BF16)
        sum_ref[...] = jnp.zeros_like(sum_ref)
        stale_ref[...] = jnp.zeros_like(stale_ref)

    row = (lax.broadcasted_iota(jnp.int32, (16, wide), 0) + step * BUILD_BLOCK).astype(jnp.int16)

    def tile(number, carry):
        lanes = pl.ds(pl.multiple_of(number * wide, wide), wide)
        index = [index_rep[slot, :, lanes] for slot in range(slots)]
        weights = [weight_rep[slot, :, lanes] for slot in range(slots)]
        for start in range(0, BUILD_BLOCK, 16):
            here = row + jnp.int16(start)
            value = jnp.zeros((16, wide), BF16)
            for slot in range(slots):
                value = jnp.where(index[slot] == here, weights[slot], value)
            mixer_ref[start : start + 16, lanes] = value
        return carry

    lax.fori_loop(0, nodes // wide, tile, 0)

    @pl.when(step < own_blocks)
    def _():
        rows = pl.ds(pl.multiple_of(step * BUILD_BLOCK, BUILD_BLOCK), BUILD_BLOCK)
        sum_ref[...] += contract(mixer_ref[...], feat_ref[rows, :], 0, 0)

    @pl.when(step >= panel_blocks)
    def _():
        panel = cached_ref.shape[0] // skip_ref.shape[0]
        first = (step - panel_blocks) * (BUILD_BLOCK // panel)
        pieces = []
        for part in range(BUILD_BLOCK // panel):
            rows = pl.ds(pl.multiple_of((first + part) * panel, panel), panel)
            pieces.append(
                jnp.where(skip_ref[first + part] == 1, cached_ref[rows, :], jnp.zeros((), BF16))
            )
        stale_ref[...] += contract(mixer_ref[...], jnp.concatenate(pieces, axis=0), 0, 0)


def middle_kernel(
    first_row,
    skip_ref,
    weight_ref,
    arrived_ref,
    fresh_ref,
    sum_ref,
    stale_ref,
    cot_ref,
    mixer_ref,
    act_ref,
    grad_ref,
    back_ref,
    panel_ref,
    mixer,
    table,
    own_sum,
    stale,
    cot,
    act,
    grad,
    back,
    panel_back,
    in_sems,
    block_sems,
    out_sems,
):
    rows, nodes = mixer.shape
    groups = skip_ref.shape[0]
    remote, width = arrived_ref.shape
    panel = (rows - remote) // groups
    peers, peer_rows, _ = back.shape
    slots = remote // peers
    wide = 2 * BLOCK
    blocks = nodes // wide

    def load(number):
        lanes = pl.ds(number * wide, wide)
        return pltpu.make_async_copy(
            mixer_ref.at[pl.ds(first_row, rows), lanes], mixer.at[:, lanes], block_sems.at[number]
        )

    fetches = [
        pltpu.make_async_copy(source, target, in_sems.at[number])
        for number, (source, target) in enumerate(
            (
                (arrived_ref, table.at[pl.ds(0, remote)]),
                (fresh_ref, table.at[pl.ds(remote, groups * panel)]),
                (sum_ref, own_sum),
                (stale_ref, stale),
                (cot_ref, cot),
            )
        )
    ]
    for fetch in fetches[:2]:
        fetch.start()
    load(0).start()
    for fetch in fetches[2:]:
        fetch.start()
    for number in range(1, blocks):
        load(number).start()
    for fetch in fetches[:2]:
        fetch.wait()
    for group in range(groups):
        here = slice(remote + group * panel, remote + (group + 1) * panel)
        table[here, :] = jnp.where(skip_ref[group] == 1, jnp.zeros((), BF16), table[here, :])

    term = jnp.zeros((width, width), F32)
    for number in range(blocks):
        load(number).wait()
        here = slice(number * wide, (number + 1) * wide)
        product = contract(mixer[:, here], table[...], 0, 0)
        if number == 0:
            for fetch in fetches[2:]:
                fetch.wait()
        mixed = (own_sum[here, :] + product).astype(BF16)
        x = stale[here, :] + jnp.dot(mixed, weight_ref[...], preferred_element_type=F32)
        square = x * x
        bend = jnp.tanh(GELU_SCALE * x * (1.0 + GELU_CUBE * square))
        half = 0.5 * (1.0 + bend)
        act[here, :] = (x * half).astype(BF16)
        slope = half + (0.5 * GELU_SCALE) * x * (1.0 - bend * bend) * (
            1.0 + (3.0 * GELU_CUBE) * square
        )
        part = (cot[here, :].astype(F32) * slope).astype(BF16)
        grad[here, :] = part
        term += contract(mixed, part, 0, 0)

    out_copies = [
        pltpu.make_async_copy(act, act_ref, out_sems.at[0]),
        pltpu.make_async_copy(grad, grad_ref, out_sems.at[1]),
    ]
    for copy in out_copies:
        copy.start()

    high = term.astype(BF16)
    low = (term - high.astype(F32)).astype(BF16)
    across = width // LANES
    tall = width * across // peers
    for peer in range(peers):
        place = (
            slice(peer // across * tall, (peer // across + 1) * tall),
            slice(peer % across * LANES, (peer % across + 1) * LANES),
        )
        back[peer, slots:, :LANES] = high[place]
        back[peer, slots:, LANES:] = low[place]

    tall_block = remote // 2
    for start in range(0, remote, tall_block):
        value = jnp.dot(
            mixer[start : start + tall_block, :], grad[...], preferred_element_type=F32
        ).astype(BF16)
        first = start // slots
        count = tall_block // slots
        for part in range(count):
            back[first + part, :slots, :] = value[part * slots : (part + 1) * slots]
        copy = pltpu.make_async_copy(
            back.at[pl.ds(first, count)],
            back_ref.at[pl.ds(first, count)],
            out_sems.at[2 + start // tall_block],
        )
        copy.start()
        out_copies.append(copy)
    tall_block = groups * panel // 2
    for start in range(0, groups * panel, tall_block):
        value = jnp.dot(
            mixer[remote + start : remote + start + tall_block, :],
            grad[...],
            preferred_element_type=F32,
        )
        for part in range(tall_block // panel):
            panel_back[start + part * panel : start + (part + 1) * panel, :] = jnp.where(
                skip_ref[start // panel + part] == 1,
                0.0,
                value[part * panel : (part + 1) * panel],
            ).astype(BF16)
    copy = pltpu.make_async_copy(panel_back, panel_ref, out_sems.at[4])
    copy.start()
    for copy in out_copies + [copy]:
        copy.wait()


def local_kernel(mixer_ref, grad_ref, out_ref):
    out_ref[...] = jnp.dot(mixer_ref[...], grad_ref[...], preferred_element_type=F32)


def final_kernel(
    send_ref, bound_ref, local_ref, returned_ref, owner_ref, weight_ref, out_ref, owner_pair
):
    step = pl.program_id(0)
    slots = send_ref.shape[1]
    panel = bound_ref.shape[1]

    @pl.when(step == 0)
    def _():
        total = jnp.sum(owner_ref[...].astype(F32), axis=0)
        high = total.astype(BF16)
        owner_pair[:panel] = high
        owner_pair[panel:] = (total - high.astype(F32)).astype(BF16)

    row = (lax.broadcasted_iota(jnp.int32, (BLOCK, LANES), 0) + step * BLOCK).astype(jnp.int16)

    def columns(ref, start):
        index = jnp.broadcast_to(ref[:, start : start + LANES], (BLOCK, LANES)).astype(jnp.int16)
        return jnp.where(index == row, jnp.ones((), BF16), jnp.zeros((), BF16))

    pick = jnp.concatenate(
        [columns(send_ref, start) for start in range(0, slots, LANES)], axis=1
    )
    pick_owner = jnp.concatenate(
        [columns(bound_ref, start) for start in range(0, panel, LANES)] * 2, axis=1
    )
    total = (
        local_ref[...]
        + jnp.dot(pick, returned_ref[...], preferred_element_type=F32)
        + jnp.dot(pick_owner, owner_pair[...], preferred_element_type=F32)
    )
    out_ref[...] = contract(total.astype(BF16), weight_ref[...], 1, 1).astype(BF16)


def whole(dims):
    return pl.BlockSpec(dims, lambda step: (0,) * len(dims))


def vmem(mib):
    return pltpu.CompilerParams(vmem_limit_bytes=mib * MIB)


def gather_sent(send_rows, counts, features):
    peers, slots = send_rows.shape
    with jax.named_scope("gather_sent_rows"):
        return call(
            gather_kernel,
            shape((peers * slots, features.shape[1]), BF16),
            send_rows.T,
            counts.reshape(1, peers),
            features,
            in_specs=[VMEM] * 3,
            out_specs=VMEM,
            compiler_params=vmem(16),
        )


def gather_panel(bound_row, features):
    with jax.named_scope("gather_panel"):
        return call(
            panel_kernel,
            shape((bound_row.shape[1], features.shape[1]), BF16),
            bound_row,
            features,
            in_specs=[VMEM] * 2,
            out_specs=VMEM,
            compiler_params=vmem(8),
        )


def build(skip, edge_index, edge_weight, features, cached, table):
    nodes, width = features.shape
    fanout = edge_index.shape[1]
    with jax.named_scope("build_mixer"):
        return call(
            functools.partial(build_kernel, nodes // BUILD_BLOCK, (table - cached.shape[0]) // BUILD_BLOCK),
            (
                shape((table, nodes), BF16),
                shape((nodes, width), F32),
                shape((nodes, width), F32),
            ),
            skip,
            edge_index.T,
            edge_weight.T,
            features,
            cached,
            grid=(table // BUILD_BLOCK,),
            in_specs=[
                SMEM,
                whole((fanout, nodes)),
                whole((fanout, nodes)),
                whole((nodes, width)),
                whole(cached.shape),
            ],
            out_specs=[
                pl.BlockSpec((BUILD_BLOCK, nodes), lambda step: (step, 0)),
                whole((nodes, width)),
                whole((nodes, width)),
            ],
            scratch_shapes=[
                pltpu.VMEM((fanout, 16, nodes), jnp.int16),
                pltpu.VMEM((fanout, 16, nodes), BF16),
            ],
            compiler_params=vmem(44),
            cost_estimate=pl.CostEstimate(
                flops=4 * nodes * nodes * width,
                bytes_accessed=2 * table * nodes,
                transcendentals=0,
            ),
        )


def middle(skip, arrived, fresh, weight, own_sum, stale, cotangent, mixer, peers, panel_rows):
    nodes, width = own_sum.shape
    remote = arrived.shape[0]
    others = mixer.shape[0] - nodes
    back = (peers, remote // peers + width * width // (peers * LANES), width)
    with jax.named_scope("forward_and_remote_grads"):
        return call(
            functools.partial(middle_kernel, nodes),
            (
                shape((nodes, width), BF16),
                shape((nodes, width), BF16),
                shape(back, BF16),
                shape((panel_rows, width), BF16),
            ),
            skip,
            weight,
            arrived,
            fresh,
            own_sum,
            stale,
            cotangent,
            mixer,
            in_specs=[SMEM, VMEM] + [ANY] * 6,
            out_specs=[ANY] * 4,
            scratch_shapes=[
                pltpu.VMEM((others, nodes), BF16),
                pltpu.VMEM((others, width), BF16),
                pltpu.VMEM((nodes, width), F32),
                pltpu.VMEM((nodes, width), F32),
                pltpu.VMEM((nodes, width), BF16),
                pltpu.VMEM((nodes, width), BF16),
                pltpu.VMEM((nodes, width), BF16),
                pltpu.VMEM(back, BF16),
                pltpu.VMEM((panel_rows, width), BF16),
                pltpu.SemaphoreType.DMA((5,)),
                pltpu.SemaphoreType.DMA((nodes // (2 * BLOCK),)),
                pltpu.SemaphoreType.DMA((5,)),
            ],
            compiler_params=vmem(56),
        )


def own_grads(mixer, grad_pre):
    nodes, width = grad_pre.shape
    with jax.named_scope("own_grads"):
        return call(
            local_kernel,
            shape((nodes, width), F32),
            mixer,
            grad_pre,
            grid=(nodes // (2 * BLOCK),),
            in_specs=[
                pl.BlockSpec((2 * BLOCK, nodes), lambda step: (step, 0)),
                whole((nodes, width)),
            ],
            out_specs=pl.BlockSpec((2 * BLOCK, width), lambda step: (step, 0)),
            compiler_params=vmem(44),
            cost_estimate=pl.CostEstimate(
                flops=2 * nodes * nodes * width, bytes_accessed=2 * nodes * nodes, transcendentals=0
            ),
        )


def finish(send_row, bound_row, local_grad, returned, owner_grad, weight):
    nodes, width = local_grad.shape
    panel = bound_row.shape[1]
    with jax.named_scope("add_returned_rows"):
        return call(
            final_kernel,
            shape((nodes, width), BF16),
            send_row,
            bound_row,
            local_grad,
            returned,
            owner_grad,
            weight,
            grid=(nodes // BLOCK,),
            in_specs=[
                whole(send_row.shape),
                whole((1, panel)),
                pl.BlockSpec((BLOCK, width), lambda step: (step, 0)),
                whole(returned.shape),
                whole(owner_grad.shape),
                whole((width, width)),
            ],
            out_specs=pl.BlockSpec((BLOCK, width), lambda step: (step, 0)),
            scratch_shapes=[pltpu.VMEM((2 * panel, width), BF16)],
            compiler_params=vmem(16),
        )


def exchange(values, axis):
    return lax.all_to_all(values, axis, split_axis=0, concat_axis=0, tiled=True)


def everyone(part, axis):
    return exchange(jnp.broadcast_to(part[None], (lax.axis_size(axis),) + part.shape), axis)


def shards(
    features,
    weight,
    cotangent,
    edge_index,
    edge_weight,
    send_rows,
    counts,
    boundary,
    skip_flags,
    cached_panels,
):
    nodes, width = features.shape
    peers = lax.axis_size("dom")
    groups = lax.axis_size("grp")
    slots = send_rows.shape[1]
    panel = boundary.shape[0]
    remote = peers * slots
    table = nodes + remote + groups * panel
    bound_row = boundary.reshape(1, panel)
    skip = skip_flags.reshape(groups)

    own_panel = gather_panel(bound_row, features)
    fresh = lax.all_gather(own_panel, "grp", axis=0, tiled=True)
    skip, fresh = lax.optimization_barrier((skip, fresh))
    outgoing = gather_sent(send_rows, counts, features)
    arrived = exchange(outgoing.reshape(peers, slots, width), "dom").reshape(remote, width)
    mixer, own_sum, stale = build(
        skip,
        edge_index,
        edge_weight,
        features,
        cached_panels.reshape(groups * panel, width),
        table,
    )
    activated, grad_pre, back, panel_grad = middle(
        skip, arrived, fresh, weight, own_sum, stale, cotangent, mixer, peers, groups * panel
    )
    owner_grad = lax.psum_scatter(
        panel_grad.reshape(groups, panel, width), "grp", scatter_dimension=0, tiled=True
    )
    returned = exchange(back, "dom")
    local_grad = own_grads(mixer, grad_pre)
    extra = back.shape[1] - slots
    live = lax.broadcasted_iota(jnp.int32, send_rows.shape, 1) < counts[:, None]
    send_row = jnp.pad(
        jnp.where(live, send_rows, -1), ((0, 0), (0, extra)), constant_values=-1
    ).reshape(1, peers * (slots + extra))
    returned, local_grad, send_row = lax.optimization_barrier((returned, local_grad, send_row))

    pairs = returned[:, slots:, :].astype(F32)
    part = jnp.sum(pairs[:, :, :LANES] + pairs[:, :, LANES:], axis=0)
    part = jnp.sum(everyone(part, "grp"), axis=0) * (1.0 / math.sqrt(nodes * peers * groups))
    across = width // LANES
    tall = part.shape[0]
    weight_grad = (
        everyone(part, "dom")
        .reshape(peers // across, across, tall, LANES)
        .transpose(0, 2, 1, 3)
        .reshape(width, width)
    )

    feature_grad = finish(
        send_row, bound_row, local_grad, returned.reshape(-1, width), owner_grad, weight
    )
    return (activated, feature_grad, weight_grad)


def solution(mesh):
    in_specs = (
        P(("dom", "grp"), None),
        P(),
        P(("dom", "grp"), None),
        P(("dom", "grp"), None),
        P(("dom", "grp"), None),
        P(("dom", "grp"), None),
        P(("dom", "grp")),
        P(("dom", "grp")),
        P("dom", None),
        P("dom", None, None, None),
    )
    out_specs = (P(("dom", "grp"), None), P(("dom", "grp"), None), P())
    return jax.shard_map(shards, mesh=mesh, in_specs=in_specs, out_specs=out_specs, check_vma=False)
```
